256 devices in a mesh: row: 8 (over z_lo, core), col: 32 (over y, z_hi, x).
Axes of the slice: x: 4, y: 4, z: 8 (z_hi: 2, z_lo: 4; z = z_hi * 4 + z_lo), core: 2. Of those that a mesh axis runs over, the one named last changes fastest.
Arguments:
- amplitudes: bfloat16 [8, 512, 4096], P(None, 'col', 'row'), may hold values from -6 to 6
- integrals: bfloat16 [8, 4096, 32768], P('row', None, 'col'), may hold values from -0.125 to 0.125
- bare: bfloat16 [8, 512, 32768], P('row', None, 'col'), may hold values from -6 to 6
- cd_count: int32 [8], replicated, may hold values from 1 to 4096, 20480 in all
- ij_orbitals: int32 [8, 2, 512], P('row'), may hold values from 0 to 199
- ab_orbitals: int32 [8, 2, 32768], P('row', None, 'col'), may hold values from 0 to 1799
- occ_energy: float32 [200], replicated, may hold values from -2 to -0.5
- vir_energy: float32 [1800], replicated, may hold values from 0.5 to 3
Outputs:
- updated: float32 [8, 512, 32768], P('row', None, 'col')
The draws below stay inside these ranges and needn't reach their ends.
Inputs may be any that keep to these rules, and one draw needn't show every extreme that they name: Each irrep's live pairs cd are the first cd_count of its 4096 slots; some irrep has all 4096, and the counts sum to 20480.
All inputs are finite; a program needn't handle non-finite values.
Results may differ from the reference program's by a relative error of at most 0.0003.
Values may be sent and summed in bfloat16 or wider, within the bound.
No kernel may reach another device: no remote copies, remote signals or barrier semaphores. Data moves between devices by JAX's collectives and lax.ppermute only.
A program may use at most 64 MiB of HBM per device.

```python
import math
import jax
import jax.numpy as jnp
import numpy as np
from jax import lax

NOCC = 200
NVIR = 1800
IRREPS = 8
CDB = 4096
IJB = 512
ABB = 32768


def plant(entries, stream_key, least, top_value):
    place = [jax.random.randint(jax.random.fold_in(stream_key, axis), (), 0, length) for axis, length in enumerate(entries.shape)]
    widest = entries.shape.index(max(entries.shape))
    beside = place[:widest] + [(place[widest] + 1) % entries.shape[widest]] + place[widest + 1:]
    return entries.at[tuple(place)].set(least).at[tuple(beside)].set(top_value)


def steps_of(own_key, extent, pieces, least, top_value):
    loudness, own = 1.0, jax.random.fold_in(own_key, 6)
    for dim, blocks in pieces:
        heights = jnp.exp(jax.random.uniform(jax.random.fold_in(own, dim), (blocks,), jnp.float32, least / len(pieces), top_value / len(pieces)))
        loudness = loudness * jnp.repeat(heights, extent[dim] // blocks).reshape([-1 if axis == dim else 1 for axis in range(len(extent))])
    return loudness


def length_profile(count, total, limit, slope):
    loads = [(1 << 20) // math.isqrt(grade ** slope) + 1 for grade in range(2, count + 1)]
    surplus, given = total - limit - (count - 1), [1] * (count - 1)
    while surplus > 0:
        movable = [i for i in range(count - 1) if given[i] < limit]
        pool, remaining = sum([loads[i] for i in movable]), surplus
        for i in movable:
            addition = min(limit - given[i], max(1, remaining * loads[i] // pool), surplus)
            given[i] = given[i] + addition
            surplus = surplus - addition
    return np.array([limit] + given)


def ragged_sizes(rng, number_of, total, bound, skew):
    if number_of == 2:
        one = jax.random.randint(rng, (), max(1, total - bound), min(bound, total - 1) + 1)
        return jnp.stack([one, total - one])
    lengths = jnp.asarray(length_profile(number_of, total, bound, skew), jnp.int32)
    pairs = (number_of - 1) // 2
    source_of, sink = lengths[1:1 + 2 * pairs:2], lengths[2:2 + 2 * pairs:2]
    margin = jnp.minimum(source_of - 1, bound - sink)
    shifted = jax.random.randint(jax.random.fold_in(rng, 1), (pairs,), 0, 1 << 20) % (margin + 1)
    lengths = lengths.at[1:1 + 2 * pairs:2].set(source_of - shifted).at[2:2 + 2 * pairs:2].set(sink + shifted)
    return lengths[jax.random.permutation(jax.random.fold_in(rng, 2), number_of)]


def bell_draw(stream_key, extent, spread, reach, pieces=(), kind=jnp.bfloat16):
    array = spread * jax.random.normal(stream_key, extent, jnp.float32)
    if pieces:
        array = array * steps_of(stream_key, extent, pieces, -0.22, 0.18)
    return jnp.clip(array, -reach, reach).astype(kind)


def setup_inputs(seed: int = 0) -> dict:
    seeds = jax.random.split(jax.random.key(seed), 9)
    return {
        "amplitudes": bell_draw(seeds[0], (IRREPS, IJB, CDB), 1.0, 6.0, ((1, 32), (2, 8))),
        "integrals": bell_draw(seeds[1], (IRREPS, CDB, ABB), (CDB // 2) ** -0.5, 0.125, ((0, 8), (2, 32))),
        "bare": bell_draw(seeds[2], (IRREPS, IJB, ABB), 1.0, 6.0, ((0, 8), (2, 32))),
        "cd_count": ragged_sizes(seeds[3], IRREPS, 5 * CDB, CDB, 2).astype(jnp.int32),
        "ij_orbitals": plant(jax.random.randint(seeds[4], (IRREPS, 2, IJB), 0, NOCC), jax.random.fold_in(seeds[4], 1), 0, NOCC - 1).astype(jnp.int32),
        "ab_orbitals": plant(jax.random.randint(seeds[5], (IRREPS, 2, ABB), 0, NVIR), jax.random.fold_in(seeds[5], 1), 0, NVIR - 1).astype(jnp.int32),
        "occ_energy": jnp.clip(jax.random.uniform(seeds[6], (NOCC,), jnp.float32, -2.0, -0.5), -2.0, -0.5),
        "vir_energy": jnp.clip(jax.random.uniform(seeds[7], (NVIR,), jnp.float32, 0.5, 3.0), 0.5, 3.0),
    }


def reference(amplitudes, integrals, bare, cd_count, ij_orbitals, ab_orbitals, occ_energy, vir_energy):
    positions = jnp.arange(amplitudes.shape[2], dtype=jnp.int32)

    def one_block(inputs):
        amp_block, int_block, count = inputs
        live_amps = jnp.where(positions[None, :] < count, amp_block, jnp.zeros_like(amp_block))
        return jnp.dot(live_amps, int_block, preferred_element_type=jnp.float32)

    ladder = lax.map(one_block, (amplitudes, integrals, cd_count))
    residual = bare.astype(jnp.float32) + 0.5 * ladder
    occ_sum = jnp.take(occ_energy, ij_orbitals[:, 0, :]) + jnp.take(occ_energy, ij_orbitals[:, 1, :])
    vir_sum = jnp.take(vir_energy, ab_orbitals[:, 0, :]) + jnp.take(vir_energy, ab_orbitals[:, 1, :])
    return residual / (vir_sum[:, None, :] - occ_sum[:, :, None])
```

```python
import functools

import jax
import jax.numpy as jnp
from jax import lax
from jax.experimental import pallas as pl
from jax.experimental.pallas import tpu as pltpu
from jax.sharding import PartitionSpec as P

NY, NZ, NX = 4, 2, 4
TILE = 256


def moves(axis, shift):
    pairs = []
    for y in range(NY):
        for z in range(NZ):
            for x in range(NX):
                ty, tz, tx = y, z, x
                if axis == "y":
                    ty = (y + shift) % NY
                elif axis == "x":
                    tx = (x + shift) % NX
                else:
                    tz = (z + shift) % NZ
                pairs.append(((y * NZ + z) * NX + x, (ty * NZ + tz) * NX + tx))
    return pairs


def send(block, axis, shift):
    return lax.ppermute(block, "col", moves(axis, shift))


def near(block, axis):
    back = send(block, axis, 1)
    ahead = send(block, axis, -1)
    far = send(block, axis, 2)
    return jnp.stack([block, back, ahead, far])


def wide(blocks, axis):
    back = send(blocks, axis, 1)
    ahead = send(blocks, axis, -1)
    far_low = send(back[:2], axis, 1)
    far_high = send(ahead[2:], axis, -1)
    return [(blocks, 0, 0), (back, 3, 0), (ahead, 1, 0), (far_low, 2, 0), (far_high, 2, 2)]


NEAR = (0, 3, 1, 2)


def ladder_kernel(layout, place_ref, *refs):
    count = len(layout)
    pieces = refs[:count]
    integrals_ref, bare_ref, ij_ref, ab_ref, occ_ref, vir_ref, out_ref, live_ref, occ_col_ref = refs[count:]

    @pl.when(pl.program_id(0) == 0)
    def _():
        y, z, x = place_ref[0], place_ref[1], place_ref[2]
        for ref, (zs, dy0, dx0, panel, kind) in zip(pieces, layout):
            for k in range(ref.shape[0]):
                if kind == "xy":
                    dy, dx = dy0, NEAR[dx0 + k]
                else:
                    dy, dx = NEAR[dy0 + k], dx0
                row = (((y + dy) % NY) * NZ + (z + zs) % NZ) * NX + (x + dx) % NX
                row = pl.multiple_of(row * 16, 16)
                for p in range(ref.shape[1]):
                    live_ref[pl.ds(row, 16), (panel + p) * 512 : (panel + p + 1) * 512] = ref[k, p]
        for s in range(4):
            occ = jnp.zeros((8, 128), jnp.float32)
            for side in range(2):
                index = jnp.broadcast_to(ij_ref[0, side : side + 1, s * 128 : (s + 1) * 128], (8, 128))
                occ = occ + pick(occ_ref, index)
            occ_col_ref[s * 128 : (s + 1) * 128, :] = jnp.broadcast_to(occ[:1], (128, 128)).T

    ladder = jnp.dot(live_ref[...], integrals_ref[0], preferred_element_type=jnp.float32)
    for s in range(TILE // 128):
        cols = slice(s * 128, (s + 1) * 128)
        vir = jnp.zeros((8, 128), jnp.float32)
        for side in range(2):
            vir = vir + pick(vir_ref, jnp.broadcast_to(ab_ref[0, side : side + 1, cols], (8, 128)))
        residual = bare_ref[0, :, cols].astype(jnp.float32) + 0.5 * ladder[:, cols]
        out_ref[0, :, cols] = residual / (vir[:1] - occ_col_ref[...])


def pick(table_ref, index):
    rows = table_ref.shape[0]
    high, low = index >> 7, index & 127
    got = jnp.zeros((8, 128), jnp.float32)
    for r in range(rows):
        row = jnp.broadcast_to(table_ref[r : r + 1, :], (8, 128))
        got = jnp.where(high == r, jnp.take_along_axis(row, low, axis=1), got)
    return got


def on_device(
    amplitudes, integrals, bare, cd_count, ij_orbitals, ab_orbitals, occ_energy, vir_energy
):
    width = amplitudes.shape[2]
    positions = lax.axis_index("row") * width + jnp.arange(width, dtype=jnp.int32)
    live = jnp.where(
        positions[None, None, :] < cd_count[:, None, None], amplitudes, jnp.zeros_like(amplitudes)
    )
    own = lax.all_to_all(live, "row", split_axis=0, concat_axis=0, tiled=True)
    other = send(own, "z", 1)
    pieces, layout = [], []
    for zs, block in ((0, own), (1, other)):
        for part, dy_first in ((0, False), (1, True)):
            half = block[part * 4 : part * 4 + 4]
            first, second = ("y", "x") if dy_first else ("x", "y")
            for array, shift, begin in wide(near(half, first), second):
                pieces.append(array)
                if dy_first:
                    layout.append((zs, begin, shift, part * 4, "yx"))
                else:
                    layout.append((zs, shift, begin, part * 4, "xy"))
    occ_table = jnp.pad(occ_energy, (0, 56)).reshape(2, 128)
    vir_table = jnp.pad(vir_energy, (0, 120)).reshape(15, 128)
    col = lax.axis_index("col")
    place = jnp.stack([col // (NZ * NX), (col // NX) % NZ, col % NX]).astype(jnp.int32)

    def whole(array):
        return pl.BlockSpec(array.shape, lambda n, place, r=array.ndim: (0,) * r)

    return pl.pallas_call(
        functools.partial(ladder_kernel, tuple(layout)),
        grid_spec=pltpu.PrefetchScalarGridSpec(
            num_scalar_prefetch=1,
            grid=(1024 // TILE,),
            in_specs=[whole(p) for p in pieces]
            + [
                pl.BlockSpec((1, 4096, TILE), lambda n, place: (0, 0, n)),
                pl.BlockSpec((1, 512, TILE), lambda n, place: (0, 0, n)),
                whole(ij_orbitals),
                pl.BlockSpec((1, 2, TILE), lambda n, place: (0, 0, n)),
                whole(occ_table),
                whole(vir_table),
            ],
            out_specs=pl.BlockSpec((1, 512, TILE), lambda n, place: (0, 0, n)),
            scratch_shapes=[pltpu.VMEM((512, 4096), jnp.bfloat16), pltpu.VMEM((512, 128), jnp.float32)],
        ),
        out_shape=jax.ShapeDtypeStruct((1, 512, 1024), jnp.float32),
        compiler_params=pltpu.CompilerParams(vmem_limit_bytes=48 * 1024 * 1024),
    )(place, *pieces, integrals, bare, ij_orbitals, ab_orbitals, occ_table, vir_table)


def solution(mesh):
    return jax.shard_map(
        on_device,
        mesh=mesh,
        in_specs=(
            P(None, "col", "row"),
            P("row", None, "col"),
            P("row", None, "col"),
            P(),
            P("row", None, None),
            P("row", None, "col"),
            P(),
            P(),
        ),
        out_specs=P("row", None, "col"),
        check_vma=False,
    )
```

```python
import functools

import jax
import jax.numpy as jnp
from jax import lax
from jax.experimental import pallas as pl
from jax.experimental.pallas import tpu as pltpu
from jax.sharding import Mesh, PartitionSpec as P

ROW, COL = ("zlo", "core"), ("y", "zhi", "x")
TILE = 256
TILES = 1024 // TILE
NEAR = (0, 3, 1, 2)


def send(block, axis, shift):
    return lax.ppermute(block, axis, [(i, (i + shift) % 4) for i in range(4)])


def near(block, axis):
    back = send(block, axis, 1)
    ahead = send(block, axis, -1)
    far = send(block, axis, 2)
    return jnp.stack([block, back, ahead, far])


def live_kernel(counts_ref, amplitudes_ref, keep_ref, pass_ref):
    core = lax.axis_index("core")
    width = amplitudes_ref.shape[2]
    first = (lax.axis_index("zlo") * 2 + core) * width
    position = first + lax.broadcasted_iota(jnp.int32, (16, width), 1)
    for z in range(4):
        for out_ref, irrep in ((keep_ref, z * 2 + core), (pass_ref, z * 2 + 1 - core)):
            block = amplitudes_ref[irrep]
            out_ref[z] = jnp.where(position < counts_ref[irrep], block, jnp.zeros_like(block))


def pick(table_ref, index):
    high, low = index >> 7, index & 127
    got = jnp.zeros((8, 128), jnp.float32)
    for r in range(table_ref.shape[0]):
        row = jnp.broadcast_to(table_ref[r : r + 1, :], (8, 128))
        got = jnp.where(high == r, jnp.take_along_axis(row, low, axis=1), got)
    return got


def groups_of(pieces):
    out = []
    for number, (half, distance, slots) in enumerate(pieces):
        for k, slot in enumerate(slots):
            dy, dx = (distance, NEAR[slot]) if half == 0 else (NEAR[slot], distance)
            out.append((number, k, half, dy, dx))
    return out


OWN = groups_of([(h, 0, (0, 1, 2, 3)) for h in (0, 1)])
BESIDE = groups_of([(h, d, (0, 1, 2, 3)) for h in (0, 1) for d in (3, 1)])
FAR = groups_of([(h, 2, s) for h in (0, 1) for s in ((0, 1), (2, 3))])


def rows_of(half, dy, dx):
    y, x, z = lax.axis_index("y"), lax.axis_index("x"), lax.axis_index("zhi")
    return pl.ds(pl.multiple_of((((y + dy) % 4 * 2 + (z + half) % 2) * 4 + (x + dx) % 4) * 16, 16), 16)


def update(groups, refs, held_ref, bare_ref, occ_sum_ref, vir_sum_ref, out_ref, live_ref, stage_ref, sem, ready=None):
    core = lax.axis_index("core")
    for g, (number, k, _, _, _) in enumerate(groups):
        for z in range(4):
            for c in range(2):
                panel = pl.multiple_of((z * 2 + (core + c) % 2) * 512, 512)
                live_ref[g * 16 : (g + 1) * 16, pl.ds(panel, 512)] = refs[number][k, z, c]
    copies = []
    for n in range(TILES):
        tile = slice(n * TILE, (n + 1) * TILE)
        if ready is not None:
            ready(n)
        ladder = jnp.dot(live_ref[...], held_ref[:, tile], preferred_element_type=jnp.float32)
        for g, (_, _, half, dy, dx) in enumerate(groups):
            rows = rows_of(half, dy, dx)
            for s in range(TILE // 128):
                cols = slice(n * TILE + s * 128, n * TILE + (s + 1) * 128)
                part = ladder[g * 16 : (g + 1) * 16, s * 128 : (s + 1) * 128]
                residual = bare_ref[0, rows, cols].astype(jnp.float32) + 0.5 * part
                stage_ref[g * 16 : (g + 1) * 16, cols] = residual / (vir_sum_ref[:1, cols] - occ_sum_ref[rows, :])
        for g, (_, _, half, dy, dx) in enumerate(groups):
            copy = pltpu.make_async_copy(
                stage_ref.at[pl.ds(g * 16, 16), pl.ds(n * TILE, TILE)],
                out_ref.at[0, rows_of(half, dy, dx), pl.ds(n * TILE, TILE)],
                sem.at[n, g],
            )
            copy.start()
            copies.append(copy)
    for copy in copies:
        copy.wait()


def own_kernel(*refs):
    (integrals_ref, bare_ref, ij_ref, ab_ref, occ_ref, vir_ref) = refs[2:8]
    (out_ref, held_ref, occ_sum_ref, vir_sum_ref, live_ref, stage_ref, sem, load_sem) = refs[8:]
    loads = []
    for n in range(TILES):
        tile = pl.ds(n * TILE, TILE)
        loads.append(pltpu.make_async_copy(integrals_ref.at[0, :, tile], held_ref.at[:, tile], load_sem.at[n]))
        loads[-1].start()
    for s in range(4):
        cols = slice(s * 128, (s + 1) * 128)
        occ = jnp.zeros((8, 128), jnp.float32)
        for side in range(2):
            occ = occ + pick(occ_ref, jnp.broadcast_to(ij_ref[0, side : side + 1, cols], (8, 128)))
        occ_sum_ref[cols, :] = jnp.broadcast_to(occ[:1], (128, 128)).T
    for s in range(8):
        cols = slice(s * 128, (s + 1) * 128)
        vir = jnp.zeros((8, 128), jnp.float32)
        for side in range(2):
            vir = vir + pick(vir_ref, jnp.broadcast_to(ab_ref[0, side : side + 1, cols], (8, 128)))
        vir_sum_ref[:, cols] = vir
    update(
        OWN, refs[:2], held_ref, bare_ref, occ_sum_ref, vir_sum_ref, out_ref, live_ref, stage_ref, sem,
        ready=lambda n: loads[n].wait(),
    )


def more_kernel(groups, *refs):
    count = len(refs) - 9
    held_ref, bare_ref, occ_sum_ref, vir_sum_ref, _, out_ref, live_ref, stage_ref, sem = refs[count:]
    update(groups, refs[:count], held_ref, bare_ref, occ_sum_ref, vir_sum_ref, out_ref, live_ref, stage_ref, sem)


IN_VMEM = pl.BlockSpec(memory_space=pltpu.VMEM)
IN_HBM = pl.BlockSpec(memory_space=pl.ANY)
PARAMS = pltpu.CompilerParams(vmem_limit_bytes=16 * 1024 * 1024)
RESULT = jax.ShapeDtypeStruct((1, 512, 1024), jnp.float32)


def in_vmem(array):
    return pltpu.with_memory_space_constraint(array, pltpu.VMEM)


def scratch(groups):
    rows = len(groups) * 16
    return [
        pltpu.VMEM((rows, 4096), jnp.bfloat16),
        pltpu.VMEM((rows, 1024), jnp.float32),
        pltpu.SemaphoreType.DMA((TILES, len(groups))),
    ]


def more(groups, pieces, held, bare, occ_sum, vir_sum, begun):
    count = len(pieces) + 4
    return pl.pallas_call(
        functools.partial(more_kernel, groups),
        in_specs=[IN_VMEM] * count + [IN_HBM],
        out_specs=IN_HBM,
        out_shape=RESULT,
        scratch_shapes=scratch(groups),
        input_output_aliases={count: 0},
        compiler_params=PARAMS,
    )(*[in_vmem(p) for p in pieces], held, bare, occ_sum, vir_sum, begun)


def on_device(
    amplitudes, integrals, bare, cd_count, ij_orbitals, ab_orbitals, occ_energy, vir_energy
):
    width = amplitudes.shape[2]
    piece = pltpu.VMEM((4, 16, width), amplitudes.dtype)
    kept, passed = pl.pallas_call(
        live_kernel,
        out_shape=(piece, piece),
        in_specs=[pl.BlockSpec(memory_space=pltpu.SMEM), IN_VMEM],
        out_specs=(IN_VMEM, IN_VMEM),
    )(cd_count, amplitudes)
    given = lax.ppermute(passed, "core", [(0, 1), (1, 0)])
    own = lax.all_to_all(
        jnp.stack([kept, given], axis=1), "zlo", split_axis=0, concat_axis=0, tiled=True
    )
    other = lax.ppermute(own, "zhi", [(0, 1), (1, 0)])
    stacks, beside, far = [], [], []
    for block, one, two in ((own, "x", "y"), (other, "y", "x")):
        blocks = near(block, one)
        back = send(blocks, two, 1)
        ahead = send(blocks, two, -1)
        stacks.append(blocks)
        beside += [back, ahead]
        far += [send(back[:2], two, 1), send(ahead[2:], two, -1)]

    occ_table = jnp.pad(occ_energy, (0, 56)).reshape(2, 128)
    vir_table = jnp.pad(vir_energy, (0, 120)).reshape(15, 128)
    bare = in_vmem(bare)
    begun, held, occ_sum, vir_sum = pl.pallas_call(
        own_kernel,
        in_specs=[IN_VMEM] * 2 + [IN_HBM] + [IN_VMEM] * 5,
        out_specs=[IN_HBM, IN_VMEM, IN_VMEM, IN_VMEM],
        out_shape=(
            RESULT,
            pltpu.VMEM((4096, 1024), jnp.bfloat16),
            pltpu.VMEM((512, 128), jnp.float32),
            pltpu.VMEM((8, 1024), jnp.float32),
        ),
        scratch_shapes=scratch(OWN) + [pltpu.SemaphoreType.DMA((TILES,))],
        compiler_params=PARAMS,
    )(
        *[in_vmem(p) for p in stacks],
        pltpu.with_memory_space_constraint(integrals, pltpu.HBM),
        bare, ij_orbitals, ab_orbitals, occ_table, vir_table,
    )
    begun = more(BESIDE, beside, held, bare, occ_sum, vir_sum, begun)
    return more(FAR, far, held, bare, occ_sum, vir_sum, begun)


def solution(mesh):
    split = Mesh(mesh.devices.reshape(4, 2, 4, 2, 4), ("zlo", "core", "y", "zhi", "x"))
    return jax.shard_map(
        on_device,
        mesh=split,
        in_specs=(
            P(None, COL, ROW),
            P(ROW, None, COL),
            P(ROW, None, COL),
            P(),
            P(ROW, None, None),
            P(ROW, None, COL),
            P(),
            P(),
        ),
        out_specs=P(ROW, None, COL),
        check_vma=False,
    )
```

```python
import functools

import jax
import jax.numpy as jnp
from jax import lax
from jax.experimental import pallas as pl
from jax.experimental.pallas import tpu as pltpu
from jax.sharding import Mesh, PartitionSpec as P

ROW, COL = ("zlo", "core"), ("y", "zhi", "x")
TILE = 256
TILES = 1024 // TILE
STEP = 64
NEAR = (0, 3, 1, 2)


def send(block, axis, shift):
    return lax.ppermute(block, axis, [(i, (i + shift) % 4) for i in range(4)])


def near(block, axis):
    back = send(block, axis, 1)
    ahead = send(block, axis, -1)
    far = send(block, axis, 2)
    return jnp.stack([block, back, ahead, far])


def pick(table_ref, index):
    high, low = index >> 7, index & 127
    got = jnp.zeros((8, 128), jnp.float32)
    for r in range(table_ref.shape[0]):
        row = jnp.broadcast_to(table_ref[r : r + 1, :], (8, 128))
        got = jnp.where(high == r, jnp.take_along_axis(row, low, axis=1), got)
    return got


def groups_of(pieces):
    out = []
    for number, (half, distance, slots) in enumerate(pieces):
        for k, slot in enumerate(slots):
            dy, dx = (distance, NEAR[slot]) if half == 0 else (NEAR[slot], distance)
            out.append((number, k, half, dy, dx))
    return out


OWN = groups_of([(h, 0, (0, 1, 2, 3)) for h in (0, 1)])
BESIDE = groups_of([(h, d, (0, 1, 2, 3)) for h in (0, 1) for d in (3, 1)])
FAR = groups_of([(h, 2, s) for h in (0, 1) for s in ((0, 1), (2, 3))])


def rows_of(half, dy, dx):
    y, x, z = lax.axis_index("y"), lax.axis_index("x"), lax.axis_index("zhi")
    return pl.ds(pl.multiple_of((((y + dy) % 4 * 2 + (z + half) % 2) * 4 + (x + dx) % 4) * 16, 16), 16)


def update(groups, refs, held_ref, bare_ref, occ_sum_ref, vir_sum_ref, out_ref, live_ref, stage_ref, sem, ready=None):
    for g, (number, k, _, _, _) in enumerate(groups):
        for p in range(8):
            live_ref[g * 16 : (g + 1) * 16, p * 512 : (p + 1) * 512] = refs[number][k, p]
    copies = []
    for n in range(TILES):
        tile = slice(n * TILE, (n + 1) * TILE)
        if ready is not None:
            ready(n)
        ladder = jnp.dot(live_ref[...], held_ref[:, tile], preferred_element_type=jnp.float32)
        for g, (_, _, half, dy, dx) in enumerate(groups):
            rows = rows_of(half, dy, dx)
            for s in range(TILE // 128):
                cols = slice(n * TILE + s * 128, n * TILE + (s + 1) * 128)
                part = ladder[g * 16 : (g + 1) * 16, s * 128 : (s + 1) * 128]
                residual = bare_ref[0, rows, cols].astype(jnp.float32) + 0.5 * part
                stage_ref[g * 16 : (g + 1) * 16, cols] = residual / (vir_sum_ref[:1, cols] - occ_sum_ref[rows, :])
        for g, (_, _, half, dy, dx) in enumerate(groups):
            copy = pltpu.make_async_copy(
                stage_ref.at[pl.ds(g * 16, 16), pl.ds(n * TILE, TILE)],
                out_ref.at[0, rows_of(half, dy, dx), pl.ds(n * TILE, TILE)],
                sem.at[n, g],
            )
            copy.start()
            copies.append(copy)
    for copy in copies:
        copy.wait()


def own_kernel(*refs):
    (counts_ref, integrals_ref, bare_ref, ij_ref, ab_ref, occ_ref, vir_ref) = refs[2:9]
    (out_ref, held_ref, occ_sum_ref, vir_sum_ref, live_ref, stage_ref, sem, load_sem) = refs[9:]
    loads = []
    for n in range(TILES):
        tile = pl.ds(n * TILE, TILE)
        loads.append(pltpu.make_async_copy(integrals_ref.at[0, :, tile], held_ref.at[:, tile], load_sem.at[n]))
        loads[-1].start()
    for s in range(4):
        cols = slice(s * 128, (s + 1) * 128)
        occ = jnp.zeros((8, 128), jnp.float32)
        for side in range(2):
            occ = occ + pick(occ_ref, jnp.broadcast_to(ij_ref[0, side : side + 1, cols], (8, 128)))
        occ_sum_ref[cols, :] = jnp.broadcast_to(occ[:1], (128, 128)).T
    for s in range(8):
        cols = slice(s * 128, (s + 1) * 128)
        vir = jnp.zeros((8, 128), jnp.float32)
        for side in range(2):
            vir = vir + pick(vir_ref, jnp.broadcast_to(ab_ref[0, side : side + 1, cols], (8, 128)))
        vir_sum_ref[:, cols] = vir
    count = counts_ref[lax.axis_index(ROW)]

    def ready(n):
        loads[n].wait()
        tile = slice(n * TILE, (n + 1) * TILE)
        edge = count // STEP
        blank = jnp.zeros((STEP, TILE), held_ref.dtype)

        @pl.when(count < 4096)
        def _():
            rows = pl.ds(pl.multiple_of(edge * STEP, STEP), STEP)
            slots = edge * STEP + lax.broadcasted_iota(jnp.int32, (STEP, TILE), 0)
            held_ref[rows, tile] = jnp.where(slots < count, held_ref[rows, tile], blank)

        @pl.loop(edge + 1, 4096 // STEP)
        def _(step):
            held_ref[pl.ds(pl.multiple_of(step * STEP, STEP), STEP), tile] = blank

    update(
        OWN, refs[:2], held_ref, bare_ref, occ_sum_ref, vir_sum_ref, out_ref, live_ref, stage_ref, sem,
        ready=ready,
    )


def more_kernel(groups, *refs):
    count = len(refs) - 9
    held_ref, bare_ref, occ_sum_ref, vir_sum_ref, _, out_ref, live_ref, stage_ref, sem = refs[count:]
    update(groups, refs[:count], held_ref, bare_ref, occ_sum_ref, vir_sum_ref, out_ref, live_ref, stage_ref, sem)


def split_kernel(back_ref, ahead_ref, after_ref, low_ref, high_ref):
    low_ref[...] = back_ref[:2]
    high_ref[...] = ahead_ref[2:]


IN_VMEM = pl.BlockSpec(memory_space=pltpu.VMEM)
IN_SMEM = pl.BlockSpec(memory_space=pltpu.SMEM)
IN_HBM = pl.BlockSpec(memory_space=pl.ANY)
PARAMS = pltpu.CompilerParams(vmem_limit_bytes=16 * 1024 * 1024)
SMALL = pltpu.CompilerParams(vmem_limit_bytes=2 * 1024 * 1024)
RESULT = jax.ShapeDtypeStruct((1, 512, 1024), jnp.float32)


def in_vmem(array):
    return pltpu.with_memory_space_constraint(array, pltpu.VMEM)


def scratch(groups):
    rows = len(groups) * 16
    return [
        pltpu.VMEM((rows, 4096), jnp.bfloat16),
        pltpu.VMEM((rows, 1024), jnp.float32),
        pltpu.SemaphoreType.DMA((TILES, len(groups))),
    ]


def more(groups, pieces, held, bare, occ_sum, vir_sum, begun):
    count = len(pieces) + 4
    return pl.pallas_call(
        functools.partial(more_kernel, groups),
        in_specs=[IN_VMEM] * count + [IN_HBM],
        out_specs=IN_HBM,
        out_shape=RESULT,
        scratch_shapes=scratch(groups),
        input_output_aliases={count: 0},
        compiler_params=PARAMS,
    )(*[in_vmem(p) for p in pieces], held, bare, occ_sum, vir_sum, begun)


def relayed(back, ahead, after):
    half = pltpu.VMEM((2, *back.shape[1:]), back.dtype)
    return pl.pallas_call(
        split_kernel,
        in_specs=[IN_VMEM] * 2 + [IN_HBM],
        out_specs=(IN_VMEM, IN_VMEM),
        out_shape=(half, half),
        compiler_params=SMALL,
    )(in_vmem(back), in_vmem(ahead), after)


def on_device(
    amplitudes, integrals, bare, cd_count, ij_orbitals, ab_orbitals, occ_energy, vir_energy
):
    own = lax.all_to_all(amplitudes, ROW, split_axis=0, concat_axis=0, tiled=True)
    other = lax.ppermute(own, "zhi", [(0, 1), (1, 0)])
    stacks, beside = [], []
    for block, one, two in ((own, "x", "y"), (other, "y", "x")):
        blocks = near(block, one)
        back = send(blocks, two, 1)
        ahead = send(blocks, two, -1)
        stacks.append(blocks)
        beside += [back, ahead]

    occ_table = jnp.pad(occ_energy, (0, 56)).reshape(2, 128)
    vir_table = jnp.pad(vir_energy, (0, 120)).reshape(15, 128)
    bare = in_vmem(bare)
    begun, held, occ_sum, vir_sum = pl.pallas_call(
        own_kernel,
        in_specs=[IN_VMEM] * 2 + [IN_SMEM, IN_HBM] + [IN_VMEM] * 5,
        out_specs=[IN_HBM, IN_VMEM, IN_VMEM, IN_VMEM],
        out_shape=(
            RESULT,
            pltpu.VMEM((4096, 1024), jnp.bfloat16),
            pltpu.VMEM((512, 128), jnp.float32),
            pltpu.VMEM((8, 1024), jnp.float32),
        ),
        scratch_shapes=scratch(OWN) + [pltpu.SemaphoreType.DMA((TILES,))],
        compiler_params=PARAMS,
    )(
        *[in_vmem(p) for p in stacks],
        cd_count,
        pltpu.with_memory_space_constraint(integrals, pltpu.HBM),
        bare, ij_orbitals, ab_orbitals, occ_table, vir_table,
    )
    far = []
    for half, axis in enumerate(("y", "x")):
        low, high = relayed(beside[half * 2], beside[half * 2 + 1], vir_sum)
        far += [send(low, axis, 1), send(high, axis, -1)]
    begun = more(BESIDE, beside, held, bare, occ_sum, vir_sum, begun)
    return more(FAR, far, held, bare, occ_sum, vir_sum, begun)


def solution(mesh):
    split = Mesh(mesh.devices.reshape(4, 2, 4, 2, 4), ("zlo", "core", "y", "zhi", "x"))
    return jax.shard_map(
        on_device,
        mesh=split,
        in_specs=(
            P(None, COL, ROW),
            P(ROW, None, COL),
            P(ROW, None, COL),
            P(),
            P(ROW, None, None),
            P(ROW, None, COL),
            P(),
            P(),
        ),
        out_specs=P(ROW, None, COL),
        check_vma=False,
    )
```

```python
import functools

import jax
import jax.numpy as jnp
from jax import lax
from jax.experimental import pallas as pl
from jax.experimental.pallas import tpu as pltpu
from jax.sharding import Mesh, PartitionSpec as P

ROW, COL = ("zlo", "core"), ("y", "zhi", "x")
TILE = 512
TILES = 1024 // TILE
STEP = 64
NEAR = (0, 3, 1, 2)


def send(block, axis, shift):
    return lax.ppermute(block, axis, [(i, (i + shift) % 4) for i in range(4)])


def near(block, axis):
    back = send(block, axis, 1)
    ahead = send(block, axis, -1)
    far = send(block, axis, 2)
    return jnp.stack([block, back, ahead, far])


def pick(table_ref, index):
    high, low = index >> 7, index & 127
    got = jnp.zeros((8, 128), jnp.float32)
    for r in range(table_ref.shape[0]):
        row = jnp.broadcast_to(table_ref[r : r + 1, :], (8, 128))
        got = jnp.where(high == r, jnp.take_along_axis(row, low, axis=1), got)
    return got


def groups_of(pieces):
    out = []
    for number, (half, distance, slots) in enumerate(pieces):
        for k, slot in enumerate(slots):
            dy, dx = (distance, NEAR[slot]) if half == 0 else (NEAR[slot], distance)
            out.append((number, k, half, dy, dx))
    return out


OWN = groups_of([(h, 0, (0, 1, 2, 3)) for h in (0, 1)])
BESIDE = groups_of([(h, d, (0, 1, 2, 3)) for h in (0, 1) for d in (3, 1)])
FAR = groups_of([(h, 2, s) for h in (0, 1) for s in ((0, 1), (2, 3))])


def rows_of(half, dy, dx):
    y, x, z = lax.axis_index("y"), lax.axis_index("x"), lax.axis_index("zhi")
    return pl.ds(pl.multiple_of((((y + dy) % 4 * 2 + (z + half) % 2) * 4 + (x + dx) % 4) * 16, 16), 16)


def update(groups, refs, held_ref, bare_ref, occ_sum_ref, vir_sum_ref, out_ref, live_ref, stage_ref, sem, ready=None):
    for g, (number, k, _, _, _) in enumerate(groups):
        for p in range(8):
            live_ref[g * 16 : (g + 1) * 16, p * 512 : (p + 1) * 512] = refs[number][k, p]
    copies = []
    for n in range(TILES):
        tile = slice(n * TILE, (n + 1) * TILE)
        if ready is not None:
            ready(n)
        ladder = jnp.dot(live_ref[...], held_ref[:, tile], preferred_element_type=jnp.float32)
        for g, (_, _, half, dy, dx) in enumerate(groups):
            rows = rows_of(half, dy, dx)
            for s in range(TILE // 128):
                cols = slice(n * TILE + s * 128, n * TILE + (s + 1) * 128)
                part = ladder[g * 16 : (g + 1) * 16, s * 128 : (s + 1) * 128]
                residual = bare_ref[0, rows, cols].astype(jnp.float32) + 0.5 * part
                stage_ref[g * 16 : (g + 1) * 16, cols] = residual / (vir_sum_ref[:1, cols] - occ_sum_ref[rows, :])
        for g, (_, _, half, dy, dx) in enumerate(groups):
            copy = pltpu.make_async_copy(
                stage_ref.at[pl.ds(g * 16, 16), pl.ds(n * TILE, TILE)],
                out_ref.at[0, rows_of(half, dy, dx), pl.ds(n * TILE, TILE)],
                sem.at[n, g],
            )
            copy.start()
            copies.append(copy)
    for copy in copies:
        copy.wait()


def own_kernel(*refs):
    (counts_ref, integrals_ref, bare_ref, ij_ref, ab_ref, occ_ref, vir_ref) = refs[2:9]
    (out_ref, held_ref, occ_sum_ref, vir_sum_ref, live_ref, stage_ref, sem, load_sem) = refs[9:]
    loads = []
    for n in range(TILES):
        tile = pl.ds(n * TILE, TILE)
        loads.append(pltpu.make_async_copy(integrals_ref.at[0, :, tile], held_ref.at[:, tile], load_sem.at[n]))
        loads[-1].start()
    for s in range(4):
        cols = slice(s * 128, (s + 1) * 128)
        occ = jnp.zeros((8, 128), jnp.float32)
        for side in range(2):
            occ = occ + pick(occ_ref, jnp.broadcast_to(ij_ref[0, side : side + 1, cols], (8, 128)))
        occ_sum_ref[cols, :] = jnp.broadcast_to(occ[:1], (128, 128)).T
    for s in range(8):
        cols = slice(s * 128, (s + 1) * 128)
        vir = jnp.zeros((8, 128), jnp.float32)
        for side in range(2):
            vir = vir + pick(vir_ref, jnp.broadcast_to(ab_ref[0, side : side + 1, cols], (8, 128)))
        vir_sum_ref[:, cols] = vir
    count = counts_ref[lax.axis_index(ROW)]

    def ready(n):
        loads[n].wait()
        tile = slice(n * TILE, (n + 1) * TILE)
        edge = count // STEP
        blank = jnp.zeros((STEP, TILE), held_ref.dtype)

        @pl.when(count < 4096)
        def _():
            rows = pl.ds(pl.multiple_of(edge * STEP, STEP), STEP)
            slots = edge * STEP + lax.broadcasted_iota(jnp.int32, (STEP, TILE), 0)
            held_ref[rows, tile] = jnp.where(slots < count, held_ref[rows, tile], blank)

        @pl.loop(edge + 1, 4096 // STEP)
        def _(step):
            held_ref[pl.ds(pl.multiple_of(step * STEP, STEP), STEP), tile] = blank

    update(
        OWN, refs[:2], held_ref, bare_ref, occ_sum_ref, vir_sum_ref, out_ref, live_ref, stage_ref, sem,
        ready=ready,
    )


def more_kernel(groups, *refs):
    count = len(refs) - 9
    held_ref, bare_ref, occ_sum_ref, vir_sum_ref, _, out_ref, live_ref, stage_ref, sem = refs[count:]
    update(groups, refs[:count], held_ref, bare_ref, occ_sum_ref, vir_sum_ref, out_ref, live_ref, stage_ref, sem)


def split_kernel(back_ref, ahead_ref, after_ref, low_ref, high_ref):
    low_ref[...] = back_ref[:2]
    high_ref[...] = ahead_ref[2:]


IN_VMEM = pl.BlockSpec(memory_space=pltpu.VMEM)
IN_SMEM = pl.BlockSpec(memory_space=pltpu.SMEM)
IN_HBM = pl.BlockSpec(memory_space=pl.ANY)
PARAMS = pltpu.CompilerParams(vmem_limit_bytes=16 * 1024 * 1024)
SMALL = pltpu.CompilerParams(vmem_limit_bytes=2 * 1024 * 1024)
RESULT = jax.ShapeDtypeStruct((1, 512, 1024), jnp.float32)


def in_vmem(array):
    return pltpu.with_memory_space_constraint(array, pltpu.VMEM)


def scratch(groups):
    rows = len(groups) * 16
    return [
        pltpu.VMEM((rows, 4096), jnp.bfloat16),
        pltpu.VMEM((rows, 1024), jnp.float32),
        pltpu.SemaphoreType.DMA((TILES, len(groups))),
    ]


def more(groups, pieces, held, bare, occ_sum, vir_sum, begun):
    count = len(pieces) + 4
    return pl.pallas_call(
        functools.partial(more_kernel, groups),
        in_specs=[IN_VMEM] * count + [IN_HBM],
        out_specs=IN_HBM,
        out_shape=RESULT,
        scratch_shapes=scratch(groups),
        input_output_aliases={count: 0},
        compiler_params=PARAMS,
    )(*[in_vmem(p) for p in pieces], held, bare, occ_sum, vir_sum, begun)


def relayed(back, ahead, after):
    half = pltpu.VMEM((2, *back.shape[1:]), back.dtype)
    return pl.pallas_call(
        split_kernel,
        in_specs=[IN_VMEM] * 2 + [IN_HBM],
        out_specs=(IN_VMEM, IN_VMEM),
        out_shape=(half, half),
        compiler_params=SMALL,
    )(in_vmem(back), in_vmem(ahead), after)


def on_device(
    amplitudes, integrals, bare, cd_count, ij_orbitals, ab_orbitals, occ_energy, vir_energy
):
    own = lax.all_to_all(amplitudes, ROW, split_axis=0, concat_axis=0, tiled=True)
    other = lax.ppermute(own, "zhi", [(0, 1), (1, 0)])
    stacks, beside = [], []
    for block, one, two in ((own, "x", "y"), (other, "y", "x")):
        blocks = near(block, one)
        back = send(blocks, two, 1)
        ahead = send(blocks, two, -1)
        stacks.append(blocks)
        beside += [back, ahead]

    occ_table = jnp.pad(occ_energy, (0, 56)).reshape(2, 128)
    vir_table = jnp.pad(vir_energy, (0, 120)).reshape(15, 128)
    bare = in_vmem(bare)
    begun, held, occ_sum, vir_sum = pl.pallas_call(
        own_kernel,
        in_specs=[IN_VMEM] * 2 + [IN_SMEM, IN_HBM] + [IN_VMEM] * 5,
        out_specs=[IN_HBM, IN_VMEM, IN_VMEM, IN_VMEM],
        out_shape=(
            RESULT,
            pltpu.VMEM((4096, 1024), jnp.bfloat16),
            pltpu.VMEM((512, 128), jnp.float32),
            pltpu.VMEM((8, 1024), jnp.float32),
        ),
        scratch_shapes=scratch(OWN) + [pltpu.SemaphoreType.DMA((TILES,))],
        compiler_params=PARAMS,
    )(
        *[in_vmem(p) for p in stacks],
        cd_count,
        pltpu.with_memory_space_constraint(integrals, pltpu.HBM),
        bare, ij_orbitals, ab_orbitals, occ_table, vir_table,
    )
    far = []
    for half, axis in enumerate(("y", "x")):
        low, high = relayed(beside[half * 2], beside[half * 2 + 1], vir_sum)
        far += [send(low, axis, 1), send(high, axis, -1)]
    begun = more(BESIDE, beside, held, bare, occ_sum, vir_sum, begun)
    return more(FAR, far, held, bare, occ_sum, vir_sum, begun)


def solution(mesh):
    split = Mesh(mesh.devices.reshape(4, 2, 4, 2, 4), ("zlo", "core", "y", "zhi", "x"))
    return jax.shard_map(
        on_device,
        mesh=split,
        in_specs=(
            P(None, COL, ROW),
            P(ROW, None, COL),
            P(ROW, None, COL),
            P(),
            P(ROW, None, None),
            P(ROW, None, COL),
            P(),
            P(),
        ),
        out_specs=P(ROW, None, COL),
        check_vma=False,
    )
```

```python
import functools

import jax
import jax.numpy as jnp
from jax import lax
from jax.experimental import pallas as pl
from jax.experimental.pallas import tpu as pltpu
from jax.sharding import Mesh, PartitionSpec as P

ROW, COL = ("zlo", "core"), ("y", "zhi", "x")
TILE = 512
TILES = 1024 // TILE
STEP = 64
NEAR = (0, 3, 1, 2)


def send(block, axis, shift):
    return lax.ppermute(block, axis, [(i, (i + shift) % 4) for i in range(4)])


def near(block, axis):
    back = send(block, axis, 1)
    ahead = send(block, axis, -1)
    far = send(block, axis, 2)
    return jnp.stack([block, back, ahead, far])


def pick(table_ref, index):
    high, low = index >> 7, index & 127
    got = jnp.zeros((8, 128), jnp.float32)
    for r in range(table_ref.shape[0]):
        row = jnp.broadcast_to(table_ref[r : r + 1, :], (8, 128))
        got = jnp.where(high == r, jnp.take_along_axis(row, low, axis=1), got)
    return got


def groups_of(pieces):
    out = []
    for number, (half, distance, slots) in enumerate(pieces):
        for k, slot in enumerate(slots):
            dy, dx = (distance, NEAR[slot]) if half == 0 else (NEAR[slot], distance)
            out.append((number, k, half, dy, dx))
    return out


OWN = groups_of([(h, 0, (0, 1, 2, 3)) for h in (0, 1)])
BESIDE = groups_of([(h, d, (0, 1, 2, 3)) for h in (0, 1) for d in (3, 1)])
FAR = groups_of([(h, 2, s) for h in (0, 1) for s in ((0, 1), (2, 3))])


def rows_of(half, dy, dx):
    y, x, z = lax.axis_index("y"), lax.axis_index("x"), lax.axis_index("zhi")
    return pl.ds(pl.multiple_of((((y + dy) % 4 * 2 + (z + half) % 2) * 4 + (x + dx) % 4) * 16, 16), 16)


def update(groups, refs, held_ref, bare_ref, occ_sum_ref, vir_sum_ref, out_ref, live_ref, stage_ref, sem, ready=None):
    for g, (number, k, _, _, _) in enumerate(groups):
        for p in range(8):
            live_ref[g * 16 : (g + 1) * 16, p * 512 : (p + 1) * 512] = refs[number][k, p]
    copies = []
    for n in range(TILES):
        tile = slice(n * TILE, (n + 1) * TILE)
        if ready is not None:
            ready(n)
        ladder = jnp.dot(live_ref[...], held_ref[:, tile], preferred_element_type=jnp.float32)
        for g, (_, _, half, dy, dx) in enumerate(groups):
            rows = rows_of(half, dy, dx)
            for s in range(TILE // 128):
                cols = slice(n * TILE + s * 128, n * TILE + (s + 1) * 128)
                part = ladder[g * 16 : (g + 1) * 16, s * 128 : (s + 1) * 128]
                residual = bare_ref[0, rows, cols].astype(jnp.float32) + 0.5 * part
                stage_ref[g * 16 : (g + 1) * 16, cols] = residual / (vir_sum_ref[:1, cols] - occ_sum_ref[rows, :])
        for g, (_, _, half, dy, dx) in enumerate(groups):
            copy = pltpu.make_async_copy(
                stage_ref.at[pl.ds(g * 16, 16), pl.ds(n * TILE, TILE)],
                out_ref.at[0, rows_of(half, dy, dx), pl.ds(n * TILE, TILE)],
                sem.at[n, g],
            )
            copy.start()
            copies.append(copy)
    for copy in copies:
        copy.wait()


def own_kernel(*refs):
    (counts_ref, integrals_ref, bare_ref, ij_ref, ab_ref, occ_ref, vir_ref) = refs[2:9]
    (out_ref, held_ref, occ_sum_ref, vir_sum_ref, live_ref, stage_ref, sem, load_sem) = refs[9:]
    loads = []
    for n in range(TILES):
        tile = pl.ds(n * TILE, TILE)
        loads.append(pltpu.make_async_copy(integrals_ref.at[0, :, tile], held_ref.at[:, tile], load_sem.at[n]))
        loads[-1].start()
    for s in range(4):
        cols = slice(s * 128, (s + 1) * 128)
        occ = jnp.zeros((8, 128), jnp.float32)
        for side in range(2):
            occ = occ + pick(occ_ref, jnp.broadcast_to(ij_ref[0, side : side + 1, cols], (8, 128)))
        occ_sum_ref[cols, :] = jnp.broadcast_to(occ[:1], (128, 128)).T
    for s in range(8):
        cols = slice(s * 128, (s + 1) * 128)
        vir = jnp.zeros((8, 128), jnp.float32)
        for side in range(2):
            vir = vir + pick(vir_ref, jnp.broadcast_to(ab_ref[0, side : side + 1, cols], (8, 128)))
        vir_sum_ref[:, cols] = vir
    count = counts_ref[lax.axis_index(ROW)]

    def ready(n):
        loads[n].wait()
        tile = slice(n * TILE, (n + 1) * TILE)
        edge = count // STEP
        blank = jnp.zeros((STEP, TILE), held_ref.dtype)

        @pl.when(count < 4096)
        def _():
            rows = pl.ds(pl.multiple_of(edge * STEP, STEP), STEP)
            slots = edge * STEP + lax.broadcasted_iota(jnp.int32, (STEP, TILE), 0)
            held_ref[rows, tile] = jnp.where(slots < count, held_ref[rows, tile], blank)

        @pl.loop(edge + 1, 4096 // STEP)
        def _(step):
            held_ref[pl.ds(pl.multiple_of(step * STEP, STEP), STEP), tile] = blank

    update(
        OWN, refs[:2], held_ref, bare_ref, occ_sum_ref, vir_sum_ref, out_ref, live_ref, stage_ref, sem,
        ready=ready,
    )


def more_kernel(groups, *refs):
    count = len(refs) - 9
    held_ref, bare_ref, occ_sum_ref, vir_sum_ref, _, out_ref, live_ref, stage_ref, sem = refs[count:]
    update(groups, refs[:count], held_ref, bare_ref, occ_sum_ref, vir_sum_ref, out_ref, live_ref, stage_ref, sem)


def split_kernel(back_ref, ahead_ref, after_ref, low_ref, high_ref):
    low_ref[...] = back_ref[:2]
    high_ref[...] = ahead_ref[2:]


IN_VMEM = pl.BlockSpec(memory_space=pltpu.VMEM)
IN_SMEM = pl.BlockSpec(memory_space=pltpu.SMEM)
IN_HBM = pl.BlockSpec(memory_space=pl.ANY)
PARAMS = pltpu.CompilerParams(vmem_limit_bytes=16 * 1024 * 1024)
SMALL = pltpu.CompilerParams(vmem_limit_bytes=2 * 1024 * 1024)
RESULT = jax.ShapeDtypeStruct((1, 512, 1024), jnp.float32)


def in_vmem(array):
    return pltpu.with_memory_space_constraint(array, pltpu.VMEM)


def scratch(groups):
    rows = len(groups) * 16
    return [
        pltpu.VMEM((rows, 4096), jnp.bfloat16),
        pltpu.VMEM((rows, 1024), jnp.float32),
        pltpu.SemaphoreType.DMA((TILES, len(groups))),
    ]


def more(groups, pieces, held, bare, occ_sum, vir_sum, begun):
    count = len(pieces) + 4
    return pl.pallas_call(
        functools.partial(more_kernel, groups),
        in_specs=[IN_VMEM] * count + [IN_HBM],
        out_specs=IN_HBM,
        out_shape=RESULT,
        scratch_shapes=scratch(groups),
        input_output_aliases={count: 0},
        compiler_params=PARAMS,
    )(*[in_vmem(p) for p in pieces], held, bare, occ_sum, vir_sum, begun)


def relayed(back, ahead, after):
    half = pltpu.VMEM((2, *back.shape[1:]), back.dtype)
    return pl.pallas_call(
        split_kernel,
        in_specs=[IN_VMEM] * 2 + [IN_HBM],
        out_specs=(IN_VMEM, IN_VMEM),
        out_shape=(half, half),
        compiler_params=SMALL,
    )(in_vmem(back), in_vmem(ahead), after)


def on_device(
    amplitudes, integrals, bare, cd_count, ij_orbitals, ab_orbitals, occ_energy, vir_energy
):
    own = lax.all_to_all(amplitudes, ROW, split_axis=0, concat_axis=0, tiled=True)
    other = lax.ppermute(own, "zhi", [(0, 1), (1, 0)])
    stacks, beside = [], []
    for block, one, two in ((own, "x", "y"), (other, "y", "x")):
        blocks = near(block, one)
        back = send(blocks, two, 1)
        ahead = send(blocks, two, -1)
        stacks.append(blocks)
        beside += [back, ahead]

    occ_table = jnp.pad(occ_energy, (0, 56)).reshape(2, 128)
    vir_table = jnp.pad(vir_energy, (0, 120)).reshape(15, 128)
    bare = in_vmem(bare)
    begun, held, occ_sum, vir_sum = pl.pallas_call(
        own_kernel,
        in_specs=[IN_VMEM] * 2 + [IN_SMEM, IN_HBM] + [IN_VMEM] * 5,
        out_specs=[IN_HBM, IN_VMEM, IN_VMEM, IN_VMEM],
        out_shape=(
            RESULT,
            pltpu.VMEM((4096, 1024), jnp.bfloat16),
            pltpu.VMEM((512, 128), jnp.float32),
            pltpu.VMEM((8, 1024), jnp.float32),
        ),
        scratch_shapes=scratch(OWN) + [pltpu.SemaphoreType.DMA((TILES,))],
        compiler_params=PARAMS,
    )(
        *[in_vmem(p) for p in stacks],
        cd_count,
        pltpu.with_memory_space_constraint(integrals, pltpu.HBM),
        bare, ij_orbitals, ab_orbitals, occ_table, vir_table,
    )
    far = []
    for half, axis in enumerate(("y", "x")):
        back, ahead = beside[half * 2 : half * 2 + 2]
        low, high = (back[:2], ahead[2:]) if half else relayed(back, ahead, vir_sum)
        far += [send(low, axis, 1), send(high, axis, -1)]
    begun = more(BESIDE, beside, held, bare, occ_sum, vir_sum, begun)
    return more(FAR, far, held, bare, occ_sum, vir_sum, begun)


def solution(mesh):
    split = Mesh(mesh.devices.reshape(4, 2, 4, 2, 4), ("zlo", "core", "y", "zhi", "x"))
    return jax.shard_map(
        on_device,
        mesh=split,
        in_specs=(
            P(None, COL, ROW),
            P(ROW, None, COL),
            P(ROW, None, COL),
            P(),
            P(ROW, None, None),
            P(ROW, None, COL),
            P(),
            P(),
        ),
        out_specs=P(ROW, None, COL),
        check_vma=False,
    )
```
